32 devices in a mesh: grp: 4 (over y, x), dev: 8 (over z, core).
Axes of the slice: x: 2, y: 2, z: 4, core: 2. Of those that a mesh axis runs over, the one named last changes fastest.
Arguments:
- field: float32 [512, 512, 256, 4], P('dev', 'grp'), may hold values from -21 to 21
- start_basis: float32 [512, 64], replicated, may hold values from -6 to 6
Outputs:
- factor: float32 [512, 64], replicated
- core: float32 [64, 512, 256, 4], P(None, ('grp', 'dev'))
The draws below stay inside these ranges and needn't reach their ends.
All inputs are finite; a program needn't handle non-finite values.
Results may differ from the reference program's by a relative error of at most 0.0003.
Values sent between devices are 32-bit elements; how exact they have to be, the bound alone decides.
A program may use at most 192 MiB of HBM per device.

```python
import math
import jax
import jax.numpy as jnp
from jax import lax

I1 = 512
I2 = 512
I3 = 256
I4 = 4
RANK = 64
ITERS = 3


def draw_field(key, part):
    first, second = jax.random.split(key)
    noise = jax.random.truncated_normal(first, -5.0, 5.0, (I1, I2, I3, I4), jnp.float32)
    scales = jnp.exp(jax.random.uniform(second, (I1,), jnp.float32, 0.0, math.log(2.0)))
    mixed = noise + 0.4 * jnp.roll(noise, -1, axis=0)
    return scales[:, None, None, None] * mixed


def centred(rng, extent, deviation, bound, held_as=jnp.bfloat16):
    values = jax.random.normal(rng, extent, jnp.float32) * deviation
    return jnp.minimum(jnp.maximum(values, -bound), bound).astype(held_as)


def setup_inputs(seed: int = 0) -> dict:
    keys = jax.random.split(jax.random.key(seed), 3)
    return {
        "field": draw_field(jax.random.fold_in(keys[2], 71), 0),
        "start_basis": centred(keys[1], (I1, RANK), 1.0, 6.0, jnp.float32),
    }


def reference(field, start_basis):
    unfold = field.reshape(I1, I2 * I3 * I4)
    gram = jnp.dot(unfold.astype(jnp.float32), unfold.T.astype(jnp.float32), precision=lax.Precision.HIGHEST, preferred_element_type=jnp.float32)
    basis = start_basis
    for step in range(ITERS):
        image = jnp.dot(gram.astype(jnp.float32), basis.astype(jnp.float32), precision=lax.Precision.HIGHEST, preferred_element_type=jnp.float32)
        cross = jnp.dot(image.T.astype(jnp.float32), image.astype(jnp.float32), precision=lax.Precision.HIGHEST, preferred_element_type=jnp.float32)
        chol = jnp.linalg.cholesky(cross)
        basis = lax.linalg.triangular_solve(chol, image, left_side=False, lower=True, transpose_a=True)
    core = jnp.dot(basis.T.astype(jnp.float32), unfold.astype(jnp.float32), precision=lax.Precision.HIGHEST, preferred_element_type=jnp.float32)
    return (basis, core.reshape(RANK, I2, I3, I4))
```

```python
import functools

import jax
import jax.numpy as jnp
from jax import lax
from jax.experimental import pallas as pl
from jax.experimental.pallas import tpu as pltpu
from jax.sharding import PartitionSpec as P

ITERS = 3
LANES = 128
WINDOW = 3
MESH = pl.DeviceIdType.MESH
NT = (((1,), (1,)), ((), ()))


def partner(me, k):
    out, bit = me, 1
    while bit <= k:
        if k & bit:
            out = out + bit * (1 - 2 * ((me // bit) % 2))
        bit *= 2
    return out


def split(x):
    hi = x.astype(jnp.bfloat16)
    return hi, (x - hi.astype(jnp.float32)).astype(jnp.bfloat16)


def exchange_kernel(
    n, field, part, hi_out, lo_out, buf, hi, lo, send_sem, recv_sem, own_sem, flush_sem
):
    chunks, sub = buf.shape[0], buf.shape[2]
    rows = field.shape[0]
    me = lax.axis_index("dev")

    barrier = pltpu.get_barrier_semaphore()
    for k in range(1, n):
        pl.semaphore_signal(
            barrier, inc=1, device_id={"dev": partner(me, k)}, device_id_type=MESH
        )
    pl.semaphore_wait(barrier, n - 1)

    def remote(c, k, column_owner, row_owner):
        return pltpu.make_async_remote_copy(
            src_ref=field.at[:, column_owner * chunks + c],
            dst_ref=buf.at[c, pl.ds(row_owner * rows, rows)],
            send_sem=send_sem.at[c, k - 1],
            recv_sem=recv_sem.at[c, k - 1],
            device_id={"dev": partner(me, k)},
            device_id_type=MESH,
        )

    def own(c):
        return pltpu.make_async_copy(
            field.at[:, me * chunks + c], buf.at[c, pl.ds(me * rows, rows)], own_sem.at[c]
        )

    def start(c):
        for k in range(n - 1, 0, -1):
            remote(c, k, partner(me, k), me).start()
        own(c).start()

    def flush(c, slot):
        return (
            pltpu.make_async_copy(hi.at[slot], hi_out.at[c], flush_sem.at[0, slot]),
            pltpu.make_async_copy(lo.at[slot], lo_out.at[c], flush_sem.at[1, slot]),
        )

    for c in range(min(WINDOW, chunks)):
        start(c)
    part[...] = jnp.zeros_like(part)

    def step(c, carry):
        slot = c % 2
        for k in range(n - 1, 0, -1):
            remote(c, k, partner(me, k), me).wait_send()

        @pl.when(c + WINDOW < chunks)
        def _():
            start(c + WINDOW)

        @pl.when(c >= 2)
        def _():
            for copy in flush(c - 2, slot):
                copy.wait()

        own(c).wait()
        for k in range(1, n):
            remote(c, k, me, partner(me, k)).wait_recv()
        for s in range(sub):
            high, low = split(buf[c, :, s, :])
            hi[slot, :, s * LANES : (s + 1) * LANES] = high
            lo[slot, :, s * LANES : (s + 1) * LANES] = low
        for copy in flush(c, slot):
            copy.start()
        high = hi[slot]
        part[...] += 0.5 * lax.dot_general(
            high, high, NT, preferred_element_type=jnp.float32
        ) + lax.dot_general(high, lo[slot], NT, preferred_element_type=jnp.float32)
        return carry

    lax.fori_loop(0, chunks, step, 0)
    for c in range(max(chunks - 2, 0), chunks):
        for copy in flush(c, c % 2):
            copy.wait()


def exchange(field, n):
    rows, seconds, sub, lanes = field.shape
    chunks, full = seconds // n, rows * n
    wide = sub * lanes
    anywhere = pl.BlockSpec(memory_space=pl.ANY)
    return pl.pallas_call(
        functools.partial(exchange_kernel, n),
        out_shape=(
            jax.ShapeDtypeStruct((full, full), jnp.float32),
            jax.ShapeDtypeStruct((chunks, full, wide), jnp.bfloat16),
            jax.ShapeDtypeStruct((chunks, full, wide), jnp.bfloat16),
        ),
        in_specs=[anywhere],
        out_specs=(pl.BlockSpec(memory_space=pltpu.VMEM), anywhere, anywhere),
        scratch_shapes=[
            pltpu.VMEM((chunks, full, sub, lanes), jnp.float32),
            pltpu.VMEM((2, full, wide), jnp.bfloat16),
            pltpu.VMEM((2, full, wide), jnp.bfloat16),
            pltpu.SemaphoreType.DMA((chunks, n - 1)),
            pltpu.SemaphoreType.DMA((chunks, n - 1)),
            pltpu.SemaphoreType.DMA((chunks,)),
            pltpu.SemaphoreType.DMA((2, 2)),
        ],
        compiler_params=pltpu.CompilerParams(
            collective_id=0, has_side_effects=True, vmem_limit_bytes=56 * 2**20
        ),
    )(field)


def exact(left, right, dims=(((1,), (0,)), ((), ()))):
    return lax.dot_general(
        left, right, dims, precision=lax.Precision.HIGHEST, preferred_element_type=jnp.float32
    )


def inverse_cholesky(cross):
    rank = cross.shape[0]
    row = lax.broadcasted_iota(jnp.int32, (rank, 1), 0)
    here = lax.broadcasted_iota(jnp.int32, (rank, rank), 0)
    there = lax.broadcasted_iota(jnp.int32, (rank, rank), 1)
    left, right = cross, (here == there).astype(jnp.float32)
    for k in range(rank - 1):
        factor = left[:, k : k + 1] / left[k : k + 1, k : k + 1]
        factor = jnp.where(row > k, factor, 0.0)
        left = left - factor * left[k : k + 1, :]
        right = right - factor * right[k : k + 1, :]
    pivots = jnp.sum(jnp.where(here == there, left, 0.0), axis=1, keepdims=True)
    return right / jnp.sqrt(pivots)


def iterate_kernel(part, start, out):
    half = part[...]
    gram = half + half.T
    basis = start[...]
    for _ in range(ITERS):
        image = exact(basis, gram)
        cross = exact(image, image, NT)
        basis = exact(inverse_cholesky(cross), image)
    out[...] = basis


def core_kernel(basis, hi, lo, out):
    sub = out.shape[2]
    rank = basis.shape[0]
    high, low = split(basis[...])
    both = jnp.concatenate([high, low], axis=0)
    first = jnp.dot(both, hi[0], preferred_element_type=jnp.float32)
    second = jnp.dot(high, lo[0], preferred_element_type=jnp.float32)
    result = first[:rank] + first[rank:] + second
    for s in range(sub):
        out[:, 0, s, :] = result[:, s * LANES : (s + 1) * LANES]


def project(basis, hi, lo, sub):
    chunks, full, wide = hi.shape
    rank = basis.shape[0]
    block = pl.BlockSpec((1, full, wide), lambda c: (c, 0, 0))
    return pl.pallas_call(
        core_kernel,
        grid=(chunks,),
        out_shape=jax.ShapeDtypeStruct((rank, chunks, sub, LANES), jnp.float32),
        in_specs=[pl.BlockSpec((rank, full), lambda c: (0, 0)), block, block],
        out_specs=pl.BlockSpec((rank, 1, sub, LANES), lambda c: (0, c, 0, 0)),
        compiler_params=pltpu.CompilerParams(vmem_limit_bytes=40 * 2**20),
    )(basis, hi, lo)


def on_device(field, start_basis):
    n = lax.axis_size("dev")
    rows, seconds, third, fourth = field.shape
    rank = start_basis.shape[1]
    fold = third // LANES
    sub = fold * fourth
    tiles = field.reshape(rows, seconds, fold, LANES, fourth).transpose(0, 1, 2, 4, 3)
    part, hi, lo = exchange(tiles.reshape(rows, seconds, sub, LANES), n)
    part = lax.psum(part, ("grp", "dev"))
    basis = pl.pallas_call(
        iterate_kernel,
        out_shape=jax.ShapeDtypeStruct((rank, start_basis.shape[0]), jnp.float32),
        compiler_params=pltpu.CompilerParams(vmem_limit_bytes=40 * 2**20),
    )(part, start_basis.T)
    core = project(basis, hi, lo, sub)
    core = core.reshape(rank, seconds // n, fold, fourth, LANES).transpose(0, 1, 2, 4, 3)
    return basis.T, core.reshape(rank, seconds // n, third, fourth)


def solution(mesh):
    placed = (P("dev", "grp", None, None), P())
    return jax.shard_map(
        on_device,
        mesh=mesh,
        in_specs=placed,
        out_specs=(P(), P(None, ("grp", "dev"), None, None)),
        check_vma=False,
    )
```

```python
import functools

import jax
import jax.numpy as jnp
from jax import lax
from jax.experimental import pallas as pl
from jax.experimental.pallas import tpu as pltpu
from jax.sharding import PartitionSpec as P

ITERS = 3
LANES = 128
WINDOW = 3
MESH = pl.DeviceIdType.MESH
NT = (((1,), (1,)), ((), ()))


def partner(me, k):
    out, bit = me, 1
    while bit <= k:
        if k & bit:
            out = out + bit * (1 - 2 * ((me // bit) % 2))
        bit *= 2
    return out


def split(x):
    hi = x.astype(jnp.bfloat16)
    return hi, (x - hi.astype(jnp.float32)).astype(jnp.bfloat16)


def tile_index(i, j):
    return i * (i + 1) // 2 + j


def sum_kernel_stages(n, groups, acc, total, sums, landed, sem):
    me, grp = lax.axis_index("dev"), lax.axis_index("grp")
    core, chip, chips = me % 2, me // 2, n // 2
    half = acc.shape[0] // 2
    slab = half // groups
    piece = slab // chips
    used = [0]

    def send(src, dst, device_id):
        i = used[0]
        used[0] += 1
        copy = pltpu.make_async_remote_copy(
            src_ref=src, dst_ref=dst, send_sem=sem.at[0, i], recv_sem=sem.at[1, i],
            device_id=device_id, device_id_type=MESH,
        )
        copy.start()
        return copy

    def finish(copies):
        for copy in copies:
            copy.wait()

    pair = {"dev": me + 1 - 2 * core}
    others = [(grp + k) % groups for k in range(1, groups)]
    along = [(chip + k) % chips for k in range(1, chips)]
    pair_sum, grp_sum = sums
    pair_in, grp_in, chip_in = landed

    finish([send(acc.at[pl.ds((1 - core) * half, half)], pair_in, pair)])
    pair_sum[...] = acc[pl.ds(core * half, half)] + pair_in[...]
    finish([
        send(pair_sum.at[pl.ds(p * slab, slab)], grp_in.at[k], {"grp": p})
        for k, p in enumerate(others)
    ])
    value = pair_sum[pl.ds(grp * slab, slab)]
    for k in range(groups - 1):
        value = value + grp_in[k]
    grp_sum[...] = value
    finish([
        send(grp_sum.at[pl.ds(p * piece, piece)], chip_in.at[k], {"dev": p * 2 + core})
        for k, p in enumerate(along)
    ])
    value = grp_sum[pl.ds(chip * piece, piece)]
    for k in range(chips - 1):
        value = value + chip_in[k]
    base = core * half + grp * slab
    mine = pl.ds(base + chip * piece, piece)
    total[mine] = value
    finish([send(total.at[mine], total.at[mine], {"dev": p * 2 + core}) for p in along])
    mine = pl.ds(base, slab)
    finish([send(total.at[mine], total.at[mine], {"grp": p}) for p in others])
    mine = pl.ds(core * half, half)
    finish([send(total.at[mine], total.at[mine], pair)])


def exchange_kernel(
    n, groups, field, part, hi_out, lo_out, buf, hi, lo, acc, total, pair_sum, grp_sum,
    pair_in, grp_in, chip_in, send_sem, recv_sem, own_sem, flush_sem, sum_sem,
):
    chunks, full, sub = buf.shape[:3]
    rows = field.shape[0]
    me, grp = lax.axis_index("dev"), lax.axis_index("grp")

    barrier = pltpu.get_barrier_semaphore()
    for k in range(1, n):
        pl.semaphore_signal(
            barrier, inc=1, device_id={"dev": partner(me, k)}, device_id_type=MESH
        )
    for k in range(1, groups):
        pl.semaphore_signal(
            barrier, inc=1, device_id={"grp": (grp + k) % groups}, device_id_type=MESH
        )
    pl.semaphore_wait(barrier, n - 1 + groups - 1)

    def remote(c, k, column_owner, row_owner):
        return pltpu.make_async_remote_copy(
            src_ref=field.at[:, column_owner * chunks + c],
            dst_ref=buf.at[c, pl.ds(row_owner * rows, rows)],
            send_sem=send_sem.at[c, k - 1],
            recv_sem=recv_sem.at[c, k - 1],
            device_id={"dev": partner(me, k)},
            device_id_type=MESH,
        )

    def own(c):
        return pltpu.make_async_copy(
            field.at[:, me * chunks + c], buf.at[c, pl.ds(me * rows, rows)], own_sem.at[c]
        )

    def start(c):
        for k in range(n - 1, 0, -1):
            remote(c, k, partner(me, k), me).start()
        own(c).start()

    def flush(c, slot):
        return (
            pltpu.make_async_copy(hi.at[slot], hi_out.at[c], flush_sem.at[0, slot]),
            pltpu.make_async_copy(lo.at[slot], lo_out.at[c], flush_sem.at[1, slot]),
        )

    for c in range(min(WINDOW, chunks)):
        start(c)
    acc[...] = jnp.zeros_like(acc)

    def step(c, carry):
        slot = c % 2
        for k in range(n - 1, 0, -1):
            remote(c, k, partner(me, k), me).wait_send()

        @pl.when(c + WINDOW < chunks)
        def _():
            start(c + WINDOW)

        @pl.when(c >= 2)
        def _():
            for copy in flush(c - 2, slot):
                copy.wait()

        own(c).wait()
        for k in range(1, n):
            remote(c, k, me, partner(me, k)).wait_recv()
        for s in range(sub):
            high, low = split(buf[c, :, s, :])
            hi[slot, :, s * LANES : (s + 1) * LANES] = high
            lo[slot, :, s * LANES : (s + 1) * LANES] = low
        for copy in flush(c, slot):
            copy.start()
        step_rows = 2 * LANES
        for top in range(0, full, step_rows):
            own_rows, upto = pl.ds(top, step_rows), pl.ds(0, top + step_rows)
            high, all_high = hi[slot, own_rows], hi[slot, upto]
            block = lax.dot_general(high, all_high, NT, preferred_element_type=jnp.float32)
            block += lax.dot_general(
                lo[slot, own_rows], all_high, NT, preferred_element_type=jnp.float32
            )
            block += lax.dot_general(
                high, lo[slot, upto], NT, preferred_element_type=jnp.float32
            )
            for i in range(top // LANES, (top + step_rows) // LANES):
                for j in range(i + 1):
                    at = i * LANES - top
                    acc[pl.ds(tile_index(i, j) * LANES, LANES)] += block[
                        at : at + LANES, j * LANES : (j + 1) * LANES
                    ]
        return carry

    lax.fori_loop(0, chunks, step, 0)
    for c in range(max(chunks - 2, 0), chunks):
        for copy in flush(c, c % 2):
            copy.wait()
    sum_kernel_stages(
        n, groups, acc, total, (pair_sum, grp_sum), (pair_in, grp_in, chip_in), sum_sem
    )
    part[...] = total[...]


def exchange(field, n, groups):
    rows, seconds, sub, lanes = field.shape
    chunks, full = seconds // n, rows * n
    wide = sub * lanes
    chips = n // 2
    unit = 8 * 2 * groups * chips
    tiles = full // LANES
    packed = -(-tile_index(tiles, 0) * LANES // unit) * unit
    half = packed // 2
    slab = half // groups
    stages = 2 * (1 + groups - 1 + chips - 1)
    anywhere = pl.BlockSpec(memory_space=pl.ANY)
    return pl.pallas_call(
        functools.partial(exchange_kernel, n, groups),
        out_shape=(
            jax.ShapeDtypeStruct((packed, LANES), jnp.float32),
            jax.ShapeDtypeStruct((chunks, full, wide), jnp.bfloat16),
            jax.ShapeDtypeStruct((chunks, full, wide), jnp.bfloat16),
        ),
        in_specs=[anywhere],
        out_specs=(pl.BlockSpec(memory_space=pltpu.VMEM), anywhere, anywhere),
        scratch_shapes=[
            pltpu.VMEM((chunks, full, sub, lanes), jnp.float32),
            pltpu.VMEM((2, full, wide), jnp.bfloat16),
            pltpu.VMEM((2, full, wide), jnp.bfloat16),
            pltpu.VMEM((packed, LANES), jnp.float32),
            pltpu.VMEM((packed, LANES), jnp.float32),
            pltpu.VMEM((half, LANES), jnp.float32),
            pltpu.VMEM((slab, LANES), jnp.float32),
            pltpu.VMEM((half, LANES), jnp.float32),
            pltpu.VMEM((groups - 1, slab, LANES), jnp.float32),
            pltpu.VMEM((chips - 1, slab // chips, LANES), jnp.float32),
            pltpu.SemaphoreType.DMA((chunks, n - 1)),
            pltpu.SemaphoreType.DMA((chunks, n - 1)),
            pltpu.SemaphoreType.DMA((chunks,)),
            pltpu.SemaphoreType.DMA((2, 2)),
            pltpu.SemaphoreType.DMA((2, stages)),
        ],
        compiler_params=pltpu.CompilerParams(
            collective_id=0, has_side_effects=True, vmem_limit_bytes=56 * 2**20
        ),
    )(field)


def exact(left, right, dims=(((1,), (0,)), ((), ()))):
    return lax.dot_general(
        left, right, dims, precision=lax.Precision.HIGHEST, preferred_element_type=jnp.float32
    )


def inverse_cholesky(cross):
    rank = cross.shape[0]
    row = lax.broadcasted_iota(jnp.int32, (rank, 2 * rank), 0)
    here = lax.broadcasted_iota(jnp.int32, (rank, rank), 0)
    there = lax.broadcasted_iota(jnp.int32, (rank, rank), 1)
    both = jnp.concatenate([cross, (here == there).astype(jnp.float32)], axis=1)
    scales = []
    for k in range(0, rank, 8):
        columns = [
            jnp.broadcast_to(both[:, k + t : k + t + 1], both.shape) for t in range(8)
        ]
        lines = [both[k + t : k + t + 1, :] for t in range(8)]
        for t in range(8):
            at = k + t
            pivot = columns[t][at : at + 1, :]
            factor = jnp.where(row > at, columns[t] / pivot, 0.0)
            for u in range(t + 1, 8):
                columns[u] = columns[u] - factor * columns[t][k + u : k + u + 1, :]
                lines[u] = lines[u] - factor[k + u : k + u + 1, :] * lines[t]
            both = both - factor * lines[t]
            scales.append(pivot)
    pivots = jnp.concatenate(scales, axis=0)[:, :rank]
    return both[:, rank:] / jnp.sqrt(pivots)


def iterate_kernel(part, start, out):
    tiles = start.shape[1] // LANES

    def tile(i, j):
        return part[pl.ds(tile_index(i, j) * LANES, LANES)]

    gram = jnp.concatenate(
        [
            jnp.concatenate(
                [tile(i, j) if j <= i else tile(j, i).T for j in range(tiles)], axis=1
            )
            for i in range(tiles)
        ],
        axis=0,
    )
    basis = start[...]
    for _ in range(ITERS):
        image = exact(basis, gram)
        cross = exact(image, image, NT)
        basis = exact(inverse_cholesky(cross), image)
    out[...] = basis


def core_kernel(basis, hi, lo, out):
    sub = out.shape[2]
    rank = basis.shape[0]
    high, low = split(basis[...])
    both = jnp.concatenate([high, low], axis=0)
    first = jnp.dot(both, hi[0], preferred_element_type=jnp.float32)
    second = jnp.dot(high, lo[0], preferred_element_type=jnp.float32)
    result = first[:rank] + first[rank:] + second
    for s in range(sub):
        out[:, 0, s, :] = result[:, s * LANES : (s + 1) * LANES]


def project(basis, hi, lo, sub):
    chunks, full, wide = hi.shape
    rank = basis.shape[0]
    block = pl.BlockSpec((1, full, wide), lambda c: (c, 0, 0))
    return pl.pallas_call(
        core_kernel,
        grid=(chunks,),
        out_shape=jax.ShapeDtypeStruct((rank, chunks, sub, LANES), jnp.float32),
        in_specs=[pl.BlockSpec((rank, full), lambda c: (0, 0)), block, block],
        out_specs=pl.BlockSpec((rank, 1, sub, LANES), lambda c: (0, c, 0, 0)),
        compiler_params=pltpu.CompilerParams(vmem_limit_bytes=40 * 2**20),
    )(basis, hi, lo)


def on_device(field, start_basis):
    n = lax.axis_size("dev")
    rows, seconds, third, fourth = field.shape
    rank = start_basis.shape[1]
    fold = third // LANES
    sub = fold * fourth
    tiles = field.reshape(rows, seconds, fold, LANES, fourth).transpose(0, 1, 2, 4, 3)
    groups = lax.axis_size("grp")
    part, hi, lo = exchange(tiles.reshape(rows, seconds, sub, LANES), n, groups)
    basis = pl.pallas_call(
        iterate_kernel,
        out_shape=jax.ShapeDtypeStruct((rank, start_basis.shape[0]), jnp.float32),
        compiler_params=pltpu.CompilerParams(vmem_limit_bytes=40 * 2**20),
    )(part, start_basis.T)
    core = project(basis, hi, lo, sub)
    core = core.reshape(rank, seconds // n, fold, fourth, LANES).transpose(0, 1, 2, 4, 3)
    return basis.T, core.reshape(rank, seconds // n, third, fourth)


def solution(mesh):
    placed = (P("dev", "grp", None, None), P())
    return jax.shard_map(
        on_device,
        mesh=mesh,
        in_specs=placed,
        out_specs=(P(), P(None, ("grp", "dev"), None, None)),
        check_vma=False,
    )
```

```python
import functools

import jax
import jax.numpy as jnp
from jax import lax
from jax.experimental import pallas as pl
from jax.experimental.pallas import tpu as pltpu
from jax.sharding import PartitionSpec as P

ITERS = 3
LANES = 128
WINDOW = 3
MESH = pl.DeviceIdType.MESH
NT = (((1,), (1,)), ((), ()))


def partner(me, k):
    out, bit = me, 1
    while bit <= k:
        if k & bit:
            out = out + bit * (1 - 2 * ((me // bit) % 2))
        bit *= 2
    return out


def split(x):
    hi = x.astype(jnp.bfloat16)
    return hi, (x - hi.astype(jnp.float32)).astype(jnp.bfloat16)


def tile_index(i, j):
    return i * (i + 1) // 2 + j


def sum_kernel_stages(n, groups, acc, total, sums, landed, sem):
    me, grp = lax.axis_index("dev"), lax.axis_index("grp")
    core, chip, chips = me % 2, me // 2, n // 2
    half = acc.shape[0] // 2
    slab = half // groups
    piece = slab // chips
    used = [0]

    def send(src, dst, device_id):
        i = used[0]
        used[0] += 1
        copy = pltpu.make_async_remote_copy(
            src_ref=src, dst_ref=dst, send_sem=sem.at[0, i], recv_sem=sem.at[1, i],
            device_id=device_id, device_id_type=MESH,
        )
        copy.start()
        return copy

    def finish(copies):
        for copy in copies:
            copy.wait()

    pair = {"dev": me + 1 - 2 * core}
    others = [(grp + k) % groups for k in range(1, groups)]
    along = [(chip + k) % chips for k in range(1, chips)]
    pair_sum, grp_sum = sums
    pair_in, grp_in, chip_in = landed

    finish([send(acc.at[pl.ds((1 - core) * half, half)], pair_in, pair)])
    pair_sum[...] = acc[pl.ds(core * half, half)] + pair_in[...]
    finish([
        send(pair_sum.at[pl.ds(p * slab, slab)], grp_in.at[k], {"grp": p})
        for k, p in enumerate(others)
    ])
    value = pair_sum[pl.ds(grp * slab, slab)]
    for k in range(groups - 1):
        value = value + grp_in[k]
    grp_sum[...] = value
    finish([
        send(grp_sum.at[pl.ds(p * piece, piece)], chip_in.at[k], {"dev": p * 2 + core})
        for k, p in enumerate(along)
    ])
    value = grp_sum[pl.ds(chip * piece, piece)]
    for k in range(chips - 1):
        value = value + chip_in[k]
    base = core * half + grp * slab
    mine = pl.ds(base + chip * piece, piece)
    total[mine] = value
    finish([send(total.at[mine], total.at[mine], {"dev": p * 2 + core}) for p in along])
    mine = pl.ds(base, slab)
    finish([send(total.at[mine], total.at[mine], {"grp": p}) for p in others])
    mine = pl.ds(core * half, half)
    finish([send(total.at[mine], total.at[mine], pair)])


def exchange_kernel(
    n, groups, field, part, hi_out, lo_out, buf, hi, lo, acc, total, pair_sum, grp_sum,
    pair_in, grp_in, chip_in, send_sem, recv_sem, own_sem, flush_sem, sum_sem,
):
    chunks, full, sub = buf.shape[:3]
    rows = field.shape[0]
    me, grp = lax.axis_index("dev"), lax.axis_index("grp")

    barrier = pltpu.get_barrier_semaphore()
    for k in range(1, n):
        pl.semaphore_signal(
            barrier, inc=1, device_id={"dev": partner(me, k)}, device_id_type=MESH
        )
    for k in range(1, groups):
        pl.semaphore_signal(
            barrier, inc=1, device_id={"grp": (grp + k) % groups}, device_id_type=MESH
        )
    pl.semaphore_wait(barrier, n - 1 + groups - 1)

    def remote(c, k, column_owner, row_owner):
        return pltpu.make_async_remote_copy(
            src_ref=field.at[:, column_owner * chunks + c],
            dst_ref=buf.at[c, pl.ds(row_owner * rows, rows)],
            send_sem=send_sem.at[c, k - 1],
            recv_sem=recv_sem.at[c, k - 1],
            device_id={"dev": partner(me, k)},
            device_id_type=MESH,
        )

    def own(c):
        return pltpu.make_async_copy(
            field.at[:, me * chunks + c], buf.at[c, pl.ds(me * rows, rows)], own_sem.at[c]
        )

    def start_far(c):
        for k in range(n - 1, n // 2 - 1, -1):
            remote(c, k, partner(me, k), me).start()

    def start_near(c):
        for k in range(n // 2 - 1, 0, -1):
            remote(c, k, partner(me, k), me).start()
        own(c).start()

    def flush(c, slot):
        return (
            pltpu.make_async_copy(hi.at[slot], hi_out.at[c], flush_sem.at[0, slot]),
            pltpu.make_async_copy(lo.at[slot], lo_out.at[c], flush_sem.at[1, slot]),
        )

    for c in range(min(WINDOW, chunks)):
        start_far(c)
        if c == 0:
            start_near(0)
        if c + 1 < chunks:
            start_near(c + 1)
    acc[...] = jnp.zeros_like(acc)

    def step(c, carry):
        slot = c % 2
        for k in range(n - 1, 0, -1):
            remote(c, k, partner(me, k), me).wait_send()

        @pl.when(c + WINDOW < chunks)
        def _():
            start_far(c + WINDOW)

        @pl.when(c + WINDOW + 1 < chunks)
        def _():
            start_near(c + WINDOW + 1)

        @pl.when(c >= 2)
        def _():
            for copy in flush(c - 2, slot):
                copy.wait()

        own(c).wait()
        for k in range(1, n):
            remote(c, k, me, partner(me, k)).wait_recv()
        for s in range(sub):
            high, low = split(buf[c, :, s, :])
            hi[slot, :, s * LANES : (s + 1) * LANES] = high
            lo[slot, :, s * LANES : (s + 1) * LANES] = low
        for copy in flush(c, slot):
            copy.start()
        step_rows = 2 * LANES
        for top in range(0, full, step_rows):
            own_rows, upto = pl.ds(top, step_rows), pl.ds(0, top + step_rows)
            high, all_high = hi[slot, own_rows], hi[slot, upto]
            block = lax.dot_general(high, all_high, NT, preferred_element_type=jnp.float32)
            block += lax.dot_general(
                lo[slot, own_rows], all_high, NT, preferred_element_type=jnp.float32
            )
            block += lax.dot_general(
                high, lo[slot, upto], NT, preferred_element_type=jnp.float32
            )
            for i in range(top // LANES, (top + step_rows) // LANES):
                for j in range(i + 1):
                    at = i * LANES - top
                    acc[pl.ds(tile_index(i, j) * LANES, LANES)] += block[
                        at : at + LANES, j * LANES : (j + 1) * LANES
                    ]
        return carry

    lax.fori_loop(0, chunks, step, 0)
    sum_kernel_stages(
        n, groups, acc, total, (pair_sum, grp_sum), (pair_in, grp_in, chip_in), sum_sem
    )
    part[...] = total[...]
    for c in range(max(chunks - 2, 0), chunks):
        for copy in flush(c, c % 2):
            copy.wait()


def exchange(field, n, groups):
    rows, seconds, sub, lanes = field.shape
    chunks, full = seconds // n, rows * n
    wide = sub * lanes
    chips = n // 2
    unit = 8 * 2 * groups * chips
    tiles = full // LANES
    packed = -(-tile_index(tiles, 0) * LANES // unit) * unit
    half = packed // 2
    slab = half // groups
    stages = 2 * (1 + groups - 1 + chips - 1)
    anywhere = pl.BlockSpec(memory_space=pl.ANY)
    return pl.pallas_call(
        functools.partial(exchange_kernel, n, groups),
        out_shape=(
            jax.ShapeDtypeStruct((packed, LANES), jnp.float32),
            jax.ShapeDtypeStruct((chunks, full, wide), jnp.bfloat16),
            jax.ShapeDtypeStruct((chunks, full, wide), jnp.bfloat16),
        ),
        in_specs=[anywhere],
        out_specs=(pl.BlockSpec(memory_space=pltpu.VMEM), anywhere, anywhere),
        scratch_shapes=[
            pltpu.VMEM((chunks, full, sub, lanes), jnp.float32),
            pltpu.VMEM((2, full, wide), jnp.bfloat16),
            pltpu.VMEM((2, full, wide), jnp.bfloat16),
            pltpu.VMEM((packed, LANES), jnp.float32),
            pltpu.VMEM((packed, LANES), jnp.float32),
            pltpu.VMEM((half, LANES), jnp.float32),
            pltpu.VMEM((slab, LANES), jnp.float32),
            pltpu.VMEM((half, LANES), jnp.float32),
            pltpu.VMEM((groups - 1, slab, LANES), jnp.float32),
            pltpu.VMEM((chips - 1, slab // chips, LANES), jnp.float32),
            pltpu.SemaphoreType.DMA((chunks, n - 1)),
            pltpu.SemaphoreType.DMA((chunks, n - 1)),
            pltpu.SemaphoreType.DMA((chunks,)),
            pltpu.SemaphoreType.DMA((2, 2)),
            pltpu.SemaphoreType.DMA((2, stages)),
        ],
        compiler_params=pltpu.CompilerParams(
            collective_id=0, has_side_effects=True, vmem_limit_bytes=56 * 2**20
        ),
    )(field)


def exact(left, right, dims=(((1,), (0,)), ((), ()))):
    return lax.dot_general(
        left, right, dims, precision=lax.Precision.HIGHEST, preferred_element_type=jnp.float32
    )


def inverse_cholesky(cross):
    rank = cross.shape[0]
    row = lax.broadcasted_iota(jnp.int32, (rank, 2 * rank), 0)
    here = lax.broadcasted_iota(jnp.int32, (rank, rank), 0)
    there = lax.broadcasted_iota(jnp.int32, (rank, rank), 1)
    both = jnp.concatenate([cross, (here == there).astype(jnp.float32)], axis=1)
    scales = []
    for k in range(0, rank, 8):
        columns = [
            jnp.broadcast_to(both[:, k + t : k + t + 1], both.shape) for t in range(8)
        ]
        lines = [both[k + t : k + t + 1, :] for t in range(8)]
        for t in range(8):
            at = k + t
            pivot = columns[t][at : at + 1, :]
            factor = jnp.where(row > at, columns[t] / pivot, 0.0)
            for u in range(t + 1, 8):
                columns[u] = columns[u] - factor * columns[t][k + u : k + u + 1, :]
                lines[u] = lines[u] - factor[k + u : k + u + 1, :] * lines[t]
            both = both - factor * lines[t]
            scales.append(pivot)
    pivots = jnp.concatenate(scales, axis=0)[:, :rank]
    return both[:, rank:] / jnp.sqrt(pivots)


def iterate_kernel(part, start, out):
    tiles = start.shape[1] // LANES

    def tile(i, j):
        return part[pl.ds(tile_index(i, j) * LANES, LANES)]

    gram = jnp.concatenate(
        [
            jnp.concatenate(
                [tile(i, j) if j <= i else tile(j, i).T for j in range(tiles)], axis=1
            )
            for i in range(tiles)
        ],
        axis=0,
    )
    basis = start[...]
    for _ in range(ITERS):
        image = exact(basis, gram)
        cross = exact(image, image, NT)
        basis = exact(inverse_cholesky(cross), image)
    out[...] = basis


def core_kernel(basis, hi, lo, out):
    sub = out.shape[2]
    rank = basis.shape[0]
    high, low = split(basis[...])
    both = jnp.concatenate([high, low], axis=0)
    for c in range(hi.shape[0]):
        first = jnp.dot(both, hi[c], preferred_element_type=jnp.float32)
        second = jnp.dot(high, lo[c], preferred_element_type=jnp.float32)
        result = first[:rank] + first[rank:] + second
        for s in range(sub):
            out[:, c, s, :] = result[:, s * LANES : (s + 1) * LANES]


def project(basis, hi, lo, sub):
    chunks, full, wide = hi.shape
    rank = basis.shape[0]
    together = 2 if chunks % 2 == 0 else 1
    block = pl.BlockSpec((together, full, wide), lambda c: (c, 0, 0))
    return pl.pallas_call(
        core_kernel,
        grid=(chunks // together,),
        out_shape=jax.ShapeDtypeStruct((rank, chunks, sub, LANES), jnp.float32),
        in_specs=[pl.BlockSpec((rank, full), lambda c: (0, 0)), block, block],
        out_specs=pl.BlockSpec((rank, together, sub, LANES), lambda c: (0, c, 0, 0)),
        compiler_params=pltpu.CompilerParams(vmem_limit_bytes=40 * 2**20),
    )(basis, hi, lo)


def on_device(field, start_basis):
    n = lax.axis_size("dev")
    rows, seconds, third, fourth = field.shape
    rank = start_basis.shape[1]
    fold = third // LANES
    sub = fold * fourth
    tiles = field.reshape(rows, seconds, fold, LANES, fourth).transpose(0, 1, 2, 4, 3)
    groups = lax.axis_size("grp")
    part, hi, lo = exchange(tiles.reshape(rows, seconds, sub, LANES), n, groups)
    basis = pl.pallas_call(
        iterate_kernel,
        out_shape=jax.ShapeDtypeStruct((rank, start_basis.shape[0]), jnp.float32),
        compiler_params=pltpu.CompilerParams(vmem_limit_bytes=40 * 2**20),
    )(part, start_basis.T)
    core = project(basis, hi, lo, sub)
    core = core.reshape(rank, seconds // n, fold, fourth, LANES).transpose(0, 1, 2, 4, 3)
    return basis.T, core.reshape(rank, seconds // n, third, fourth)


def solution(mesh):
    placed = (P("dev", "grp", None, None), P())
    return jax.shard_map(
        on_device,
        mesh=mesh,
        in_specs=placed,
        out_specs=(P(), P(None, ("grp", "dev"), None, None)),
        check_vma=False,
    )
```
